128 devices in a mesh: expert: 16 (over y, z), dp: 8 (over x, core).
Axes of the slice: x: 4, y: 4, z: 4, core: 2. Of those that a mesh axis runs over, the one named last changes fastest.
Arguments:
- tokens: bfloat16 [8192, 4096], P(('expert', 'dp')), may hold values from -6 to 6
- routed_expert_index: int32 [8192, 8], P(('expert', 'dp')), may hold values from 0 to 95, as said below
- routing_weight: float32 [8192, 8], P(('expert', 'dp')), may hold values from 0.05 to 1
- serving_slot_expert: int32 [128], replicated, may hold values from 0 to 95, as said below
- frozen_gate_weight: bfloat16 [128, 4096, 768], P(('expert', 'dp')), may hold values from -1 to 1, as said below
- frozen_up_weight: bfloat16 [128, 4096, 768], P(('expert', 'dp')), may hold values from -1 to 1, as said below
- frozen_down_weight: bfloat16 [128, 768, 4096], P(('expert', 'dp')), may hold values from -1 to 1, as said below
- trainer_expert_order: int32 [96], replicated, may hold values from 0 to 95, each once
- trainer_adapter_rows: bfloat16 [96, 466944], P('expert'), may hold values from -2 to 2
Outputs:
- moe_out: bfloat16 [8192, 4096], P(('expert', 'dp'))
The draws below stay inside these ranges and needn't reach their ends.
Inputs may be any that keep to these rules, and one draw needn't show every extreme that they name: `routed_expert_index`: each token names 8 different experts. At most 8 of the 64 tokens of one device name any one expert, and one expert is named by exactly 8 tokens of every device. `serving_slot_expert`: every expert holds one or two slots, and exactly 32 experts hold two. `frozen_gate_weight`: slots that hold the same expert hold equal matrices. `frozen_up_weight`: slots that hold the same expert hold equal matrices. `frozen_down_weight`: slots that hold the same expert hold equal matrices.
All inputs are finite; a program needn't handle non-finite values.
Results may differ from the reference program's by a relative error of at most 0.0067.
Values may be sent and summed in bfloat16 or wider, within the bound.
No kernel may reach another device: no remote copies, remote signals or barrier semaphores. Data moves between devices by JAX's collectives and lax.ppermute only.
A program may use at most 192 MiB of HBM per device.

```python
import math
import jax
import jax.numpy as jnp
from jax import lax

MODEL_DIM = 4096
TOPK = 8
HALF_FEEDFORWARD = 768
ADAPTER_RANK = 32
TOK_DEV = 64
TOKENS = 8192
SLOTS = 128
EXPERTS = 96
HOT = 32
CAP = 8
PACK = 466944
DEVICES = 128


def layout(key):
    shuffled = jax.random.permutation(jax.random.fold_in(key, 101), EXPERTS).astype(jnp.int32)
    listed = jnp.concatenate([jnp.arange(EXPERTS, dtype=jnp.int32), shuffled[:HOT]])
    slot_order = jax.random.permutation(jax.random.fold_in(key, 102), SLOTS)
    serving_slot_expert = listed[slot_order].astype(jnp.int32)
    hot_flags = jnp.zeros((EXPERTS,), jnp.int32).at[shuffled[:HOT]].set(1)
    return (serving_slot_expert, hot_flags, shuffled[0])


def slot_matrices(key, serving_slot_expert, height, breadth, normal_scale):

    def one_matrix(expert_number):
        expert_key = jax.random.fold_in(key, expert_number)
        normal_part = jnp.clip(jax.random.normal(jax.random.fold_in(expert_key, 1), (height, breadth), jnp.float32), -4.0, 4.0)
        return (normal_part * normal_scale).astype(jnp.bfloat16)
    return lax.map(one_matrix, serving_slot_expert)


def draw_serving_slot_expert(key, part):
    serving_slot_expert, hot_flags, peak_expert = layout(key)
    return serving_slot_expert


def draw_routed_expert_index(key, part):
    serving_slot_expert, hot_flags, peak_expert = layout(key)
    key = jax.random.fold_in(key, 2)
    cold_copies = CAP // 2 + 1
    copies = jnp.where(hot_flags > 0, CAP, cold_copies)
    copies = jnp.where(jnp.arange(EXPERTS, dtype=jnp.int32) == peak_expert, 0, copies)
    entry_expert = jnp.repeat(jnp.arange(EXPERTS, dtype=jnp.int32), CAP)
    entry_rank = jnp.tile(jnp.arange(CAP, dtype=jnp.int32), EXPERTS)
    usable = entry_rank < copies[entry_expert]
    entry_total = EXPERTS * CAP
    needed = TOK_DEV * TOPK - CAP

    def one_block(block_key):
        first_key = jax.random.fold_in(block_key, 1)
        second_key = jax.random.fold_in(block_key, 2)
        third_key = jax.random.fold_in(block_key, 3)
        noise_draw = jax.random.randint(first_key, (entry_total,), 0, 1024)
        scores = jnp.where(usable, noise_draw, 1024) * entry_total + jnp.arange(entry_total, dtype=jnp.int32)
        picked = entry_expert[jnp.argsort(scores)[:needed]]
        chosen = jnp.sort(jnp.concatenate([jnp.full((CAP,), peak_expert, jnp.int32), picked]))
        id_table = chosen.reshape(TOPK, TOK_DEV).T
        id_table = id_table[jax.random.permutation(second_key, TOK_DEV)]
        jitter = jax.random.randint(third_key, (TOK_DEV, TOPK), 0, 1024) * TOPK + jnp.arange(TOPK, dtype=jnp.int32)[None, :]
        return jnp.take_along_axis(id_table, jnp.argsort(jitter, axis=1), axis=1)
    block_keys = jax.vmap(lambda block_number: jax.random.fold_in(key, block_number))(jnp.arange(DEVICES))
    return jax.vmap(one_block)(block_keys).reshape(TOKENS, TOPK).astype(jnp.int32)


def draw_frozen_gate_weight(key, part):
    serving_slot_expert, hot_flags, peak_expert = layout(key)
    key = jax.random.fold_in(key, 3)
    return slot_matrices(key, serving_slot_expert, MODEL_DIM, HALF_FEEDFORWARD, 1.0 / math.sqrt(MODEL_DIM))


def draw_frozen_up_weight(key, part):
    serving_slot_expert, hot_flags, peak_expert = layout(key)
    key = jax.random.fold_in(key, 4)
    return slot_matrices(key, serving_slot_expert, MODEL_DIM, HALF_FEEDFORWARD, 1.0 / math.sqrt(MODEL_DIM))


def draw_frozen_down_weight(key, part):
    serving_slot_expert, hot_flags, peak_expert = layout(key)
    key = jax.random.fold_in(key, 5)
    return slot_matrices(key, serving_slot_expert, HALF_FEEDFORWARD, MODEL_DIM, 1.0 / math.sqrt(HALF_FEEDFORWARD))


def draw_trainer_adapter_rows(key, part):
    key = jax.random.fold_in(key, 6)
    fan_scale = jnp.concatenate([jnp.full((2 * ADAPTER_RANK * MODEL_DIM,), 1.0 / math.sqrt(MODEL_DIM), jnp.float32), jnp.full((ADAPTER_RANK * MODEL_DIM,), 1.0 / math.sqrt(ADAPTER_RANK), jnp.float32), jnp.full((2 * ADAPTER_RANK * HALF_FEEDFORWARD,), 1.0 / math.sqrt(ADAPTER_RANK), jnp.float32), jnp.full((ADAPTER_RANK * HALF_FEEDFORWARD,), 1.0 / math.sqrt(HALF_FEEDFORWARD), jnp.float32)])
    raw_values = jnp.clip(jax.random.normal(key, (EXPERTS, PACK), jnp.float32), -4.0, 4.0)
    return (raw_values * fan_scale[None, :]).astype(jnp.bfloat16)


def levels(stream_key, extent, cuts, smallest, top_value):
    def one(axis_at, shards_of):
        heights = jax.random.uniform(jax.random.fold_in(jax.random.fold_in(stream_key, 6), axis_at), (shards_of,), jnp.float32, smallest / len(cuts), top_value / len(cuts))
        return jnp.repeat(jnp.exp(heights), extent[axis_at] // shards_of).reshape((-1,) + (1,) * (len(extent) - axis_at - 1))

    gain = one(*cuts[0])
    for cut in cuts[1:]:
        gain = gain * one(*cut)
    return gain


def centred(rng, dims, deviation, bound, split=(), kind=jnp.bfloat16):
    entries = jax.random.normal(rng, dims, jnp.float32) * deviation
    if len(split) > 0:
        entries = levels(rng, dims, split, -0.22, 0.18) * entries
    return jnp.clip(entries, min=-bound, max=bound).astype(kind)


def setup_inputs(seed: int = 0) -> dict:
    streams_of = jax.random.split(jax.random.key(seed), 10)
    tokens = centred(streams_of[0], (TOKENS, MODEL_DIM), 1.0, 6.0, ((0, 128),))
    routed_expert_index = draw_routed_expert_index(jax.random.fold_in(streams_of[9], 71), 0)
    routing_weight = jnp.clip(jnp.exp(math.log(1.0) - 2.9957323 * jax.random.uniform(streams_of[2], (TOKENS, TOPK), jnp.float32) ** levels(streams_of[2], (TOKENS, TOPK), ((0, 128),), -0.2, 0.2)), 0.05, 1.0)
    serving_slot_expert = draw_serving_slot_expert(jax.random.fold_in(streams_of[9], 71), 0)
    frozen_gate_weight = draw_frozen_gate_weight(jax.random.fold_in(streams_of[9], 71), 0)
    frozen_up_weight = draw_frozen_up_weight(jax.random.fold_in(streams_of[9], 71), 0)
    frozen_down_weight = draw_frozen_down_weight(jax.random.fold_in(streams_of[9], 71), 0)
    trainer_expert_order = jax.random.permutation(streams_of[7], EXPERTS).astype(jnp.int32)
    trainer_adapter_rows = draw_trainer_adapter_rows(jax.random.fold_in(streams_of[9], 71), 0)
    return {"tokens": tokens, "routed_expert_index": routed_expert_index, "routing_weight": routing_weight, "serving_slot_expert": serving_slot_expert, "frozen_gate_weight": frozen_gate_weight, "frozen_up_weight": frozen_up_weight, "frozen_down_weight": frozen_down_weight, "trainer_expert_order": trainer_expert_order, "trainer_adapter_rows": trainer_adapter_rows}


row_block = 256


def expert_row_block(row_segment, gate_matrix, up_matrix, down_matrix, adapter_wide_factor, adapter_narrow_factor):
    adapter_rank_value = adapter_wide_factor.shape[1]
    reduce_factor_pair = adapter_wide_factor[:2].reshape(2 * adapter_rank_value, adapter_wide_factor.shape[2])
    reduced_input = lax.dot_general(row_segment, reduce_factor_pair, (((1,), (1,)), ((), ())), preferred_element_type=jnp.float32).astype(jnp.bfloat16)
    gate_total = jnp.dot(row_segment, gate_matrix, preferred_element_type=jnp.float32) + jnp.dot(reduced_input[:, :adapter_rank_value], adapter_narrow_factor[0], preferred_element_type=jnp.float32)
    up_total = jnp.dot(row_segment, up_matrix, preferred_element_type=jnp.float32) + jnp.dot(reduced_input[:, adapter_rank_value:], adapter_narrow_factor[1], preferred_element_type=jnp.float32)
    hidden_state = (jax.nn.silu(gate_total) * up_total).astype(jnp.bfloat16)
    reduced_down_input = lax.dot_general(hidden_state, adapter_narrow_factor[2], (((1,), (1,)), ((), ())), preferred_element_type=jnp.float32).astype(jnp.bfloat16)
    projected_output = jnp.dot(hidden_state, down_matrix, preferred_element_type=jnp.float32) + jnp.dot(reduced_down_input, adapter_wide_factor[2], preferred_element_type=jnp.float32)
    return projected_output.astype(jnp.bfloat16)


def reference(tokens, routed_expert_index, routing_weight, serving_slot_expert, frozen_gate_weight, frozen_up_weight, frozen_down_weight, trainer_expert_order, trainer_adapter_rows):
    slot_numbers = jnp.arange(SLOTS, dtype=jnp.int32)
    hosts_match = serving_slot_expert[None, :] == jnp.arange(EXPERTS, dtype=jnp.int32)[:, None]
    first_slot = jnp.min(jnp.where(hosts_match, slot_numbers[None, :], SLOTS), axis=1).astype(jnp.int32)
    trainer_row_index = jnp.zeros((EXPERTS,), jnp.int32).at[trainer_expert_order].set(jnp.arange(EXPERTS, dtype=jnp.int32))
    flat_ids = routed_expert_index.reshape(-1)
    sorted_order = jnp.argsort(flat_ids, stable=True).astype(jnp.int32)
    sorted_order = jnp.concatenate([sorted_order, jnp.zeros((row_block,), jnp.int32)])
    expert_counts = jnp.bincount(flat_ids, length=EXPERTS).astype(jnp.int32)
    expert_starts = (jnp.cumsum(expert_counts) - expert_counts).astype(jnp.int32)
    flat_weights = routing_weight.reshape(-1)
    split_offset = 3 * ADAPTER_RANK * MODEL_DIM

    def per_expert(expert_number, result):
        slot_index = first_slot[expert_number]
        gate_matrix = frozen_gate_weight[slot_index]
        up_matrix = frozen_up_weight[slot_index]
        down_matrix = frozen_down_weight[slot_index]
        packed_adapter_row = trainer_adapter_rows[trainer_row_index[expert_number]]
        adapter_wide_factor = packed_adapter_row[:split_offset].reshape(3, ADAPTER_RANK, MODEL_DIM)
        adapter_narrow_factor = packed_adapter_row[split_offset:].reshape(3, ADAPTER_RANK, HALF_FEEDFORWARD)
        count = expert_counts[expert_number]

        def per_block(block_number, running):
            offset = (expert_starts[expert_number] + block_number * row_block).astype(jnp.int32)
            assignment = lax.dynamic_slice_in_dim(sorted_order, offset, row_block)
            token_position = assignment // TOPK
            live_rows = (block_number * row_block + jnp.arange(row_block, dtype=jnp.int32)) < count
            projected_output = expert_row_block(tokens[token_position], gate_matrix, up_matrix, down_matrix, adapter_wide_factor, adapter_narrow_factor)
            weights_live = jnp.where(live_rows, flat_weights[assignment], jnp.float32(0.0))
            return running.at[token_position].add(weights_live[:, None] * projected_output.astype(jnp.float32))

        block_total = (count + row_block - 1) // row_block
        return lax.fori_loop(0, block_total, per_block, result)

    summed = lax.fori_loop(0, EXPERTS, per_expert, jnp.zeros((TOKENS, MODEL_DIM), jnp.float32))
    return summed.astype(jnp.bfloat16)
```

```python
import functools

import jax
import jax.numpy as jnp
from jax import lax
from jax.experimental import pallas as pl
from jax.experimental.pallas import tpu as pltpu
from jax.sharding import PartitionSpec as P

bf16 = jnp.bfloat16
f32 = jnp.float32
MIB = 1 << 20

FIRST = 4
SECOND = 1
MOST = 8


def params(limit_mib):
    return pltpu.CompilerParams(vmem_limit_bytes=limit_mib * MIB)


def whole(shape):
    return pl.BlockSpec(shape, lambda *_: (0,) * len(shape))


def cut_kernel(wide_span, narrow_span, wide_total, narrow_pieces, dp_size, dp_ref, rows, out, wide_sem, narrow_sem):
    dp_index = dp_ref[0]
    copies = []
    for e in range(out.shape[0]):
        piece = e * dp_size + dp_index
        wide_at = pl.multiple_of(piece * wide_span, 128)
        narrow_at = pl.multiple_of(
            wide_total + jnp.minimum(piece, narrow_pieces - 1) * narrow_span, 128
        )
        copies.append(
            pltpu.make_async_copy(
                rows.at[:, pl.ds(wide_at, wide_span)],
                out.at[e, :, pl.ds(0, wide_span)],
                wide_sem.at[e],
            )
        )
        copies.append(
            pltpu.make_async_copy(
                rows.at[:, pl.ds(narrow_at, narrow_span)],
                out.at[e, :, pl.ds(wide_span, narrow_span)],
                narrow_sem.at[e],
            )
        )
    for copy in copies:
        copy.start()
    for copy in copies:
        copy.wait()


def cut_pieces(rows, dp_index, groups, dp_size, wide_total, wide_span, narrow_span, narrow_pieces):
    held = rows.shape[0]
    return pl.pallas_call(
        functools.partial(
            cut_kernel, wide_span, narrow_span, wide_total, narrow_pieces, dp_size
        ),
        in_specs=[
            pl.BlockSpec(memory_space=pltpu.SMEM),
            pl.BlockSpec(memory_space=pl.ANY),
        ],
        out_specs=pl.BlockSpec(memory_space=pl.ANY),
        out_shape=jax.ShapeDtypeStruct((groups, held, wide_span + narrow_span), bf16),
        scratch_shapes=[
            pltpu.SemaphoreType.DMA((groups,)),
            pltpu.SemaphoreType.DMA((groups,)),
        ],
        name="adapter_cut",
    )(dp_index.reshape(1), rows)


def pick_kernel(held, wanted, flag, pieces, out, rows):
    groups, _, span = pieces.shape
    slots = out.shape[0]
    rows[...] = jnp.zeros_like(rows)
    for e in range(groups):
        rows[8 * e : 8 * e + held, :] = pieces[e].astype(f32)
    want = wanted[...]
    place = (want // held) * 8 + want % held
    chosen = lax.broadcasted_iota(jnp.int32, (8 * groups, slots), 0) == place
    picked = lax.dot_general(
        chosen.astype(bf16),
        rows[...].astype(bf16),
        (((0,), (0,)), ((), ())),
        preferred_element_type=f32,
    )
    tail = jnp.broadcast_to(flag[...], (slots, out.shape[1] * out.shape[2] - span))
    full = jnp.concatenate([picked, tail], axis=1).astype(bf16)
    out[...] = full.reshape(out.shape)


def pick_pieces(pieces, wanted, flag, slots):
    groups, held, span = pieces.shape
    units = 32
    return pl.pallas_call(
        functools.partial(pick_kernel, held),
        out_shape=jax.ShapeDtypeStruct((slots, units, 128), bf16),
        scratch_shapes=[pltpu.VMEM((8 * groups, span), f32)],
        compiler_params=params(40),
        name="adapter_pick",
    )(wanted.reshape(1, slots), flag.reshape(1, 1), pieces)


def placement(ids, info):
    tokens = ids.shape[0]
    named = ids[:, 0:1] == info[0:1, :]
    for k in range(1, ids.shape[1]):
        named = named | (ids[:, k : k + 1] == info[0:1, :])
    before = lax.broadcasted_iota(jnp.int32, (tokens, tokens), 0) > lax.broadcasted_iota(
        jnp.int32, (tokens, tokens), 1
    )
    rank = jnp.dot(before.astype(bf16), named.astype(bf16), preferred_element_type=f32)
    return named & (rank == info[1:2, :].astype(f32))


def dispatch_kernel(ids, info, tokens, out):
    fills = placement(ids[...], info[...]).astype(bf16)
    sent = lax.dot_general(
        fills, tokens[...], (((0,), (0,)), ((), ())), preferred_element_type=f32
    )
    out[...] = sent.astype(bf16).reshape(out.shape)


def dispatch(ids, info, tokens, slots, cell):
    rows = info.shape[1]
    block = 128
    steps = rows // block
    count, width = tokens.shape
    out_block = (slots // steps,) + cell
    return pl.pallas_call(
        dispatch_kernel,
        grid=(steps,),
        in_specs=[
            whole(ids.shape),
            pl.BlockSpec((2, block), lambda i: (0, i)),
            whole(tokens.shape),
        ],
        out_specs=pl.BlockSpec(out_block, lambda i: (i, 0, 0)),
        out_shape=jax.ShapeDtypeStruct((slots,) + cell, bf16),
        compiler_params=params(32),
        cost_estimate=pl.CostEstimate(
            flops=2 * rows * count * width, bytes_accessed=2 * rows * width, transcendentals=0
        ),
        name="token_dispatch",
    )(ids, info, tokens)


def expert_kernel(
    up_steps,
    x_ref,
    gate_ref,
    up_ref,
    down_ref,
    wide,
    narrow,
    out,
    x,
    shrunk,
    hidden,
    shrunk_down,
):
    step = pl.program_id(0)
    rank = wide.shape[0] // 3
    tile = gate_ref.shape[1]

    @pl.when(step == 0)
    def _():
        x[...] = x_ref[...].reshape(x.shape)
        shrunk[...] = lax.dot_general(
            x[...],
            wide[0 : 2 * rank, :],
            (((1,), (1,)), ((), ())),
            preferred_element_type=f32,
        ).astype(bf16)

    for f in range(up_steps):

        @pl.when(step == f)
        def _():
            at = slice(f * tile, (f + 1) * tile)
            gate = jnp.dot(x[...], gate_ref[...], preferred_element_type=f32) + jnp.dot(
                shrunk[:, :rank], narrow[0:rank, at], preferred_element_type=f32
            )
            up = jnp.dot(x[...], up_ref[...], preferred_element_type=f32) + jnp.dot(
                shrunk[:, rank:], narrow[rank : 2 * rank, at], preferred_element_type=f32
            )
            hidden[:, at] = (gate / (1.0 + jnp.exp(-gate)) * up).astype(bf16)

    @pl.when(step == up_steps)
    def _():
        shrunk_down[...] = lax.dot_general(
            hidden[...],
            narrow[2 * rank :, :],
            (((1,), (1,)), ((), ())),
            preferred_element_type=f32,
        ).astype(bf16)

    @pl.when(step >= up_steps)
    def _():
        width = down_ref.shape[1]
        at = pl.multiple_of((step - up_steps) * width, width)
        total = jnp.dot(hidden[...], down_ref[...], preferred_element_type=f32) + jnp.dot(
            shrunk_down[...], wide[2 * rank :, pl.ds(at, width)], preferred_element_type=f32
        )
        out[...] = total.astype(bf16).reshape(out.shape)


def expert(x, gate, up, down, wide, narrow):
    model, units = gate.shape
    slots = x.shape[0]
    rows = x.size // model
    tile = 256
    up_steps = units // tile
    halves = x.shape[2] != model
    down_width = 1024
    down_steps = model // down_width
    rank = wide.shape[0] // 3

    def down_at(i):
        return jnp.maximum(i - up_steps, 0)

    out_rows = (rows, down_width) if halves else (slots, x.shape[1], down_width)
    out_shape = (rows, model) if halves else x.shape
    if halves:
        out_map = lambda i: (0, down_at(i))
    else:
        out_map = lambda i: (0, 0, down_at(i))
    return pl.pallas_call(
        functools.partial(expert_kernel, up_steps),
        grid=(up_steps + down_steps,),
        in_specs=[
            whole(x.shape),
            pl.BlockSpec((model, tile), lambda i: (0, jnp.minimum(i, up_steps - 1))),
            pl.BlockSpec((model, tile), lambda i: (0, jnp.minimum(i, up_steps - 1))),
            pl.BlockSpec((units, down_width), lambda i: (0, down_at(i))),
            whole(wide.shape),
            whole(narrow.shape),
        ],
        out_specs=pl.BlockSpec(out_rows, out_map),
        out_shape=jax.ShapeDtypeStruct(out_shape, bf16),
        scratch_shapes=[
            pltpu.VMEM((rows, model), bf16),
            pltpu.VMEM((rows, 2 * rank), bf16),
            pltpu.VMEM((rows, units), bf16),
            pltpu.VMEM((rows, rank), bf16),
        ],
        compiler_params=params(56),
        cost_estimate=pl.CostEstimate(
            flops=6 * rows * model * units,
            bytes_accessed=6 * model * units + 4 * rows * model,
            transcendentals=rows * units,
        ),
        name="slot_expert",
    )(x, gate, up, down, wide, narrow)


def combine_kernel(ids, weight, info, answers, *rest):
    out = rest[-1]
    fills = placement(ids[...], info[...])
    given = jnp.zeros(fills.shape, f32)
    for k in range(ids.shape[1]):
        given = given + jnp.where(ids[:, k : k + 1] == info[0:1, :], weight[:, k : k + 1], 0.0)
    given = jnp.where(fills, given, 0.0)
    high = given.astype(bf16)
    low = (given - high.astype(f32)).astype(bf16)
    both = jnp.concatenate([high, low], axis=0)
    rows = info.shape[1]
    block = answers[...].reshape(rows, out.shape[1])
    sums = jnp.dot(both, block, preferred_element_type=f32)
    count = ids.shape[0]
    total = sums[:count] + sums[count:]
    if len(rest) == 2:
        total = total + rest[0][...]
    out[...] = total.astype(out.dtype)


def combine(ids, weight, info, answers, before=None, kind=f32):
    count = ids.shape[0]
    rows = info.shape[1]
    flat = answers.ndim == 2
    model = answers.shape[-1]
    width = 1024
    if flat:
        answer_spec = pl.BlockSpec((rows, width), lambda i: (0, i))
    else:
        answer_spec = pl.BlockSpec(answers.shape[:2] + (width,), lambda i: (0, 0, i))
    total_spec = pl.BlockSpec((count, width), lambda i: (0, i))
    more = () if before is None else (before,)
    return pl.pallas_call(
        combine_kernel,
        grid=(model // width,),
        in_specs=[whole(ids.shape), whole(weight.shape), whole(info.shape), answer_spec]
        + [total_spec] * len(more),
        out_specs=total_spec,
        out_shape=jax.ShapeDtypeStruct((count, model), kind),
        compiler_params=params(32),
        cost_estimate=pl.CostEstimate(
            flops=4 * count * rows * model, bytes_accessed=2 * rows * model, transcendentals=0
        ),
        name="token_combine",
    )(ids, weight, info, answers, *more)


def body(
    tokens,
    ids,
    weight,
    serving,
    gate,
    up,
    down,
    trainer_order,
    trainer_rows,
):
    groups = lax.axis_size("expert")
    dp_size = lax.axis_size("dp")
    dp_index = lax.axis_index("dp").astype(jnp.int32)
    slots = serving.shape[0]
    experts = trainer_order.shape[0]
    held, packed = trainer_rows.shape
    count, model = tokens.shape
    units = gate.shape[2]
    rank = packed // (3 * (model + units))
    everyone = ("expert", "dp")

    slot_at = jnp.arange(slots, dtype=jnp.int32)
    same = serving[:, None] == serving[None, :]
    second = jnp.any(same & (slot_at[None, :] < slot_at[:, None]), axis=1)
    hot = jnp.sum(same.astype(jnp.int32), axis=1) > 1

    def rows_info(first, places, filled):
        place = jnp.arange(places, dtype=jnp.int32)[None, :]
        at = first + place
        ranks = jnp.where(hot[:, None], 2 * at + second[:, None].astype(jnp.int32), at)
        ranks = jnp.where(place < filled, ranks, -1)
        who = jnp.broadcast_to(serving[:, None], (slots, places))
        return jnp.stack([who.reshape(-1), ranks.reshape(-1)])

    info_a = rows_info(0, FIRST, FIRST)
    info_b = rows_info(FIRST, SECOND, SECOND)
    info_c = rows_info(FIRST + SECOND, 4, MOST - FIRST - SECOND)
    named = jnp.sum((ids.reshape(-1)[:, None] == serving[None, :]).astype(jnp.int32), axis=0)
    left_over = jnp.any((named > FIRST + SECOND) & ~hot).astype(f32)

    wide_total = 3 * rank * model
    pieces = groups * dp_size
    wide_span = wide_total // pieces
    mine = cut_pieces(
        trainer_rows, dp_index, groups, dp_size, wide_total, wide_span, units, 3 * rank
    )
    spread = lax.all_to_all(mine, "expert", split_axis=0, concat_axis=0, tiled=True)
    trainer_row = jnp.sum(
        jnp.where(
            serving[:, None] == trainer_order[None, :],
            jnp.arange(experts, dtype=jnp.int32)[None, :],
            0,
        ),
        axis=1,
    )
    picked = pick_pieces(spread, trainer_row, left_over, slots)
    factors = lax.all_to_all(picked, everyone, split_axis=0, concat_axis=0, tiled=True)
    wide_units = wide_span // 128
    span_units = (wide_span + units) // 128
    wide = factors[:, :wide_units, :].reshape(3 * rank, model)
    narrow = factors[: 3 * rank, wide_units:span_units, :].reshape(3 * rank, units)
    any_left = jnp.max(factors[:, span_units, 0].astype(f32)) > 0.0

    def there(cells):
        return lax.all_to_all(cells, everyone, split_axis=0, concat_axis=0, tiled=True)

    def run(x):
        return expert(x, gate[0], up[0], down[0], wide, narrow)

    cell_a = (FIRST, model)
    cell_b = (2, model // 2)
    in_a = there(dispatch(ids, info_a, tokens, slots, cell_a))
    in_b = there(dispatch(ids, info_b, tokens, slots, cell_b))
    back_a = there(run(in_a))
    back_b = there(run(in_b).reshape((slots,) + cell_b)).reshape(slots, model)
    total = combine(ids, weight, info_a, back_a)

    def rest():
        in_c = there(dispatch(ids, info_c, tokens, slots, cell_a))
        return combine(ids, weight, info_c, there(run(in_c)), total)

    total = lax.cond(any_left, rest, lambda: total)
    return combine(ids, weight, info_b, back_b, total, bf16)


def solution(mesh):
    split = P(("expert", "dp"), None)
    slot = P(("expert", "dp"), None, None)
    placed = (split, split, split, P(), slot, slot, slot, P(), P("expert", None))
    return jax.shard_map(body, mesh=mesh, in_specs=placed, out_specs=split, check_vma=False)
```

```python
import functools

import jax
import jax.numpy as jnp
from jax import lax
from jax.experimental import pallas as pl
from jax.experimental.pallas import tpu as pltpu
from jax.sharding import PartitionSpec as P

bf16 = jnp.bfloat16
f32 = jnp.float32
MIB = 1 << 20

PLACES = 5
MOST = 8


def params(limit_mib):
    return pltpu.CompilerParams(vmem_limit_bytes=limit_mib * MIB)


def whole(shape):
    return pl.BlockSpec(shape, lambda *_: (0,) * len(shape))


def cut_kernel(wide_rows, narrow, dp_size, limit, where, ids, serving, column, rows, out, cut, sems):
    groups, held, model = cut.shape
    dp_index = where[0]
    first_narrow = wide_rows // dp_size
    rank = wide_rows // 3
    copies = []
    for e in range(groups):
        piece = e * dp_size + dp_index
        if e < first_narrow:
            spans = [(piece * model, 0, model)]
        else:
            q = piece - wide_rows
            spans = [
                (wide_rows * model + (g * rank + q) * narrow, g * narrow, narrow) for g in range(3)
            ]
        for source, target, width in spans:
            copies.append(
                pltpu.make_async_copy(
                    rows.at[:, pl.ds(pl.multiple_of(source, 128), width)],
                    cut.at[e, :, pl.ds(target, width)],
                    sems.at[len(copies)],
                )
            )
    for copy in copies:
        copy.start()
    slots = serving.shape[1]
    named = jnp.zeros((ids.shape[0], slots), f32)
    for k in range(ids.shape[1]):
        named = named + (ids[:, k : k + 1] == serving[...]).astype(f32)
    named = jnp.sum(named, axis=0, keepdims=True)
    holders = jnp.sum((column[...] == serving[...]).astype(f32), axis=0, keepdims=True)
    over = jnp.where((named > limit) & (holders < 2.0), 1.0, 0.0)
    over = jnp.max(over, axis=1, keepdims=True)
    for e in range(first_narrow, groups):
        cut[e, :, 3 * narrow :] = jnp.broadcast_to(over, (held, model - 3 * narrow)).astype(bf16)
    for copy in copies:
        copy.wait()
    for e in range(groups):
        out[e] = cut[e].reshape(out.shape[1:])


def cut_pieces(rows, dp_index, ids, serving, limit, groups, dp_size, model, narrow, rank):
    held = rows.shape[0]
    slots = serving.shape[0]
    wide_rows = 3 * rank
    first_narrow = wide_rows // dp_size
    held_in = pl.BlockSpec(memory_space=pltpu.VMEM)
    return pl.pallas_call(
        functools.partial(cut_kernel, wide_rows, narrow, dp_size, limit),
        in_specs=[
            pl.BlockSpec(memory_space=pltpu.SMEM),
            held_in,
            held_in,
            held_in,
            pl.BlockSpec(memory_space=pltpu.HBM),
        ],
        out_specs=held_in,
        out_shape=jax.ShapeDtypeStruct((groups, held * model // 128, 128), bf16),
        scratch_shapes=[
            pltpu.VMEM((groups, held, model), bf16),
            pltpu.SemaphoreType.DMA((first_narrow + 3 * (groups - first_narrow),)),
        ],
        compiler_params=params(16),
        name="adapter_cut",
    )(dp_index.reshape(1), ids, serving.reshape(1, slots), serving.reshape(slots, 1), rows)


def pick_kernel(held, flag_at, where, wanted, pieces, cells, out, rows):
    groups = pieces.shape[0]
    model = rows.shape[1]
    slots = out.shape[0]
    rows[...] = jnp.zeros_like(rows)
    for e in range(groups):
        rows[8 * e : 8 * e + held, :] = pieces[e].reshape(held, model).astype(f32)
    want = wanted[...]
    place = (want // held) * 8 + want % held
    chosen = lax.broadcasted_iota(jnp.int32, (8 * groups, slots), 0) == place
    picked = lax.dot_general(
        chosen.astype(bf16),
        rows[...].astype(bf16),
        (((0,), (0,)), ((), ())),
        preferred_element_type=f32,
    )
    flags = jnp.max(rows[:, flag_at : flag_at + 128], axis=0, keepdims=True)
    kept = picked[:, flag_at : flag_at + 128]
    flags = jnp.where(where[0] > 0, jnp.broadcast_to(flags, kept.shape), kept)
    full = jnp.concatenate([picked[:, :flag_at], flags, picked[:, flag_at + 128 :]], axis=1)
    out[...] = full.astype(bf16).reshape(out.shape)


def pick_pieces(pieces, held, wanted, holds_flag, flag_at, cells):
    groups = pieces.shape[0]
    model = pieces.shape[1] * pieces.shape[2] // held
    slots, units, lanes = cells.shape
    block = (slots, model // lanes, lanes)
    last = units * lanes // model - 1
    return pl.pallas_call(
        functools.partial(pick_kernel, held, flag_at),
        grid=(1,),
        in_specs=[
            pl.BlockSpec(memory_space=pltpu.SMEM),
            whole((1, slots)),
            whole(pieces.shape),
            pl.BlockSpec(memory_space=pl.ANY),
        ],
        out_specs=pl.BlockSpec(block, lambda i: (0, last, 0)),
        out_shape=jax.ShapeDtypeStruct(cells.shape, bf16),
        input_output_aliases={3: 0},
        scratch_shapes=[pltpu.VMEM((8 * groups, model), f32)],
        compiler_params=params(24),
        name="adapter_pick",
    )(holds_flag.reshape(1), wanted.reshape(1, slots), pieces, cells)


def placement(ids, info):
    tokens = ids.shape[0]
    named = ids[:, 0:1] == info[0:1, :]
    for k in range(1, ids.shape[1]):
        named = named | (ids[:, k : k + 1] == info[0:1, :])
    before = lax.broadcasted_iota(jnp.int32, (tokens, tokens), 0) > lax.broadcasted_iota(
        jnp.int32, (tokens, tokens), 1
    )
    rank = jnp.dot(before.astype(bf16), named.astype(bf16), preferred_element_type=f32)
    return named & (rank == info[1:2, :].astype(f32))


def dispatch_kernel(ids, info, tokens, out):
    fills = placement(ids[...], info[0]).astype(bf16)
    sent = lax.dot_general(
        fills, tokens[...], (((0,), (0,)), ((), ())), preferred_element_type=f32
    )
    out[...] = sent.astype(bf16).reshape(out.shape)


def dispatch(ids, info, tokens):
    places, _, slots = info.shape
    count, model = tokens.shape
    return pl.pallas_call(
        dispatch_kernel,
        grid=(places,),
        in_specs=[
            whole(ids.shape),
            pl.BlockSpec((1, 2, slots), lambda j: (j, 0, 0)),
            whole(tokens.shape),
        ],
        out_specs=pl.BlockSpec((slots, model // 128, 128), lambda j: (0, j, 0)),
        out_shape=jax.ShapeDtypeStruct((slots, (places + 1) * model // 128, 128), bf16),
        compiler_params=params(24),
        cost_estimate=pl.CostEstimate(
            flops=2 * places * slots * count * model,
            bytes_accessed=2 * places * slots * model,
            transcendentals=0,
        ),
        name="token_dispatch",
    )(ids, info, tokens)


def expert_kernel(
    rank,
    cells,
    gate_hbm,
    up_hbm,
    down_hbm,
    out,
    gate,
    up,
    down,
    x,
    factors,
    shrunk,
    hidden,
    sent,
    gate_sems,
    up_sems,
    down_sems,
    out_sems,
):
    slots = cells.shape[0]
    rows, model = x.shape
    units = hidden.shape[1]
    row = model // 128
    places = rows // slots
    tile = units // gate_sems.shape[0]
    width = sent.shape[2] * 128
    up_tiles, down_tiles = units // tile, model // width

    def tile_at(i, size):
        return pl.ds(pl.multiple_of(i * size, size), size)

    def load(i, source, target, size, sems):
        at = tile_at(i, size)
        return pltpu.make_async_copy(source.at[:, at], target.at[:, at], sems.at[i])

    def load_gate(i):
        return load(i, gate_hbm, gate, tile, gate_sems)

    def load_up(i):
        return load(i, up_hbm, up, tile, up_sems)

    def load_down(i):
        return load(i, down_hbm, down, width, down_sems)

    def send(i, j):
        at = pl.ds(pl.multiple_of(j * row + i * (width // 128), 8), width // 128)
        return pltpu.make_async_copy(sent.at[j], out.at[:, at, :], out_sems.at[i * places + j])

    for i in range(up_tiles):
        load_gate(i).start()
        load_up(i).start()
    for i in range(down_tiles):
        load_down(i).start()

    factors[...] = cells[:, places * row :, :].reshape(slots, model)

    @pl.loop(0, places)
    def _(j):
        here = tile_at(j, slots)
        part = cells[:, tile_at(j, row), :].reshape(slots, model)
        x[here, :] = part
        shrunk[here, :] = lax.dot_general(
            part,
            factors[0 : 2 * rank, :],
            (((1,), (1,)), ((), ())),
            preferred_element_type=f32,
        ).astype(bf16)

    @pl.loop(0, up_tiles)
    def _(i):
        at = tile_at(i, tile)
        load_gate(i).wait()
        load_up(i).wait()
        into_gate = jnp.dot(x[...], gate[:, at], preferred_element_type=f32) + jnp.dot(
            shrunk[:, :rank], factors[3 * rank : 4 * rank, at], preferred_element_type=f32
        )
        up_at = pl.ds(pl.multiple_of(units + i * tile, tile), tile)
        into_up = jnp.dot(x[...], up[:, at], preferred_element_type=f32) + jnp.dot(
            shrunk[:, rank:], factors[3 * rank : 4 * rank, up_at], preferred_element_type=f32
        )
        hidden[:, at] = (into_gate / (1.0 + jnp.exp(-into_gate)) * into_up).astype(bf16)

    shrunk_down = lax.dot_general(
        hidden[...],
        factors[3 * rank : 4 * rank, 2 * units : 3 * units],
        (((1,), (1,)), ((), ())),
        preferred_element_type=f32,
    ).astype(bf16)

    @pl.loop(0, down_tiles)
    def _(i):
        at = tile_at(i, width)
        load_down(i).wait()
        total = jnp.dot(hidden[...], down[:, at], preferred_element_type=f32) + jnp.dot(
            shrunk_down, factors[2 * rank : 3 * rank, at], preferred_element_type=f32
        )
        for j in range(places):

            @pl.when(i > 0)
            def _():
                send(i - 1, j).wait()

            part = total[j * slots : (j + 1) * slots].astype(bf16)
            sent[j] = part.reshape(slots, width // 128, 128)
            send(i, j).start()

    for j in range(places):
        send(down_tiles - 1, j).wait()


def expert(cells, gate, up, down, rank):
    model, units = gate.shape
    slots = cells.shape[0]
    places = cells.size // model // slots - 1
    rows = slots * places
    tile, width = 256, 1024
    in_hbm = pl.BlockSpec(memory_space=pltpu.HBM)
    return pl.pallas_call(
        functools.partial(expert_kernel, rank),
        in_specs=[pl.BlockSpec(memory_space=pltpu.VMEM)] + [in_hbm] * 3,
        out_specs=in_hbm,
        out_shape=jax.ShapeDtypeStruct((slots, places * model // 128, 128), bf16),
        scratch_shapes=[
            pltpu.VMEM((model, units), bf16),
            pltpu.VMEM((model, units), bf16),
            pltpu.VMEM((units, model), bf16),
            pltpu.VMEM((rows, model), bf16),
            pltpu.VMEM((slots, model), bf16),
            pltpu.VMEM((rows, 2 * rank), bf16),
            pltpu.VMEM((rows, units), bf16),
            pltpu.VMEM((places, slots, width // 128, 128), bf16),
            pltpu.SemaphoreType.DMA((units // tile,)),
            pltpu.SemaphoreType.DMA((units // tile,)),
            pltpu.SemaphoreType.DMA((model // width,)),
            pltpu.SemaphoreType.DMA((places * (model // width),)),
        ],
        compiler_params=params(48),
        cost_estimate=pl.CostEstimate(
            flops=6 * rows * model * units,
            bytes_accessed=6 * model * units + 4 * rows * model,
            transcendentals=rows * units,
        ),
        name="slot_expert",
    )(cells, gate, up, down)


def combine_kernel(ids, weight, info, answers, *rest):
    block, out = rest[-1], rest[-2]
    count, model = out.shape
    rows, width = block.shape
    slots = answers.shape[0]
    places = rows // slots
    row = model // 128
    fills = placement(ids[...], info[...])
    given = jnp.zeros(fills.shape, f32)
    for k in range(ids.shape[1]):
        given = given + jnp.where(ids[:, k : k + 1] == info[0:1, :], weight[:, k : k + 1], 0.0)
    given = jnp.where(fills, given, 0.0)
    high = given.astype(bf16)
    low = (given - high.astype(f32)).astype(bf16)
    both = jnp.concatenate([high, low], axis=0)

    @pl.loop(0, model // width)
    def _(i):
        at = pl.ds(pl.multiple_of(i * width, width), width)
        for j in range(places):
            units = pl.ds(pl.multiple_of(j * row + i * (width // 128), 8), width // 128)
            block[j * slots : (j + 1) * slots, :] = answers[:, units, :].reshape(slots, width)
        total = jnp.dot(both, block[...], preferred_element_type=f32)
        total = total[:count] + total[count:]
        if len(rest) == 3:
            total = total + rest[0][:, at]
        out[:, at] = total.astype(out.dtype)


def combine(ids, weight, info, answers, before=None, kind=f32):
    count = ids.shape[0]
    places, _, slots = info.shape
    model = answers.size // places // slots
    held = pl.BlockSpec(memory_space=pltpu.VMEM)
    more = () if before is None else (before,)
    info = info.transpose(1, 0, 2).reshape(2, places * slots)
    return pl.pallas_call(
        combine_kernel,
        in_specs=[held] * (4 + len(more)),
        out_specs=held,
        out_shape=jax.ShapeDtypeStruct((count, model), kind),
        scratch_shapes=[pltpu.VMEM((places * slots, 1024), bf16)],
        compiler_params=params(24),
        cost_estimate=pl.CostEstimate(
            flops=4 * count * places * slots * model,
            bytes_accessed=2 * places * slots * model,
            transcendentals=0,
        ),
        name="token_combine",
    )(ids, weight, info, answers, *more)


def body(
    tokens,
    ids,
    weight,
    serving,
    gate,
    up,
    down,
    trainer_order,
    trainer_rows,
):
    groups = lax.axis_size("expert")
    dp_size = lax.axis_size("dp")
    dp_index = lax.axis_index("dp").astype(jnp.int32)
    slots = serving.shape[0]
    experts = trainer_order.shape[0]
    held, packed = trainer_rows.shape
    count, model = tokens.shape
    units = gate.shape[2]
    rank = packed // (3 * (model + units))
    everyone = ("expert", "dp")

    slot_at = jnp.arange(slots, dtype=jnp.int32)
    same = serving[:, None] == serving[None, :]
    second = jnp.any(same & (slot_at[None, :] < slot_at[:, None]), axis=1)
    hot = jnp.sum(same.astype(jnp.int32), axis=1) > 1

    def places_info(first, last):
        at = jnp.arange(first, last, dtype=jnp.int32)[:, None]
        ranks = jnp.where(hot[None, :], 2 * at + second[None, :].astype(jnp.int32), at)
        who = jnp.broadcast_to(serving[None, :], ranks.shape)
        return jnp.stack([who, ranks], axis=1)

    mine = cut_pieces(
        trainer_rows, dp_index, ids, serving, PLACES, groups, dp_size, model, units, rank
    )
    spread = lax.all_to_all(mine, "expert", split_axis=0, concat_axis=0, tiled=True)
    trainer_row = jnp.sum(
        jnp.where(
            serving[:, None] == trainer_order[None, :],
            jnp.arange(experts, dtype=jnp.int32)[None, :],
            0,
        ),
        axis=1,
    )
    holds_flag = (lax.axis_index("expert") * dp_size + dp_index >= 3 * rank).astype(jnp.int32)

    def there(cells):
        return lax.all_to_all(cells, everyone, split_axis=0, concat_axis=0, tiled=True)

    def run(info):
        cells = dispatch(ids, info, tokens)
        cells = there(pick_pieces(spread, held, trainer_row, holds_flag, 3 * units, cells))
        return cells, there(expert(cells, gate[0], up[0], down[0], rank))

    info = places_info(0, PLACES)
    cells, answers = run(info)
    flags = cells[3 * rank :, (PLACES * model + 3 * units) // 128, 0]

    def one_round():
        return combine(ids, weight, info, answers, None, bf16)

    def two_rounds():
        more = places_info(PLACES, MOST)
        return combine(ids, weight, more, run(more)[1], combine(ids, weight, info, answers), bf16)

    return lax.cond(jnp.max(flags.astype(f32)) > 0.0, two_rounds, one_round)


def solution(mesh):
    split = P(("expert", "dp"), None)
    slot = P(("expert", "dp"), None, None)
    placed = (split, split, split, P(), slot, slot, slot, P(), P("expert", None))
    return jax.shard_map(body, mesh=mesh, in_specs=placed, out_specs=split, check_vma=False)
```

```python
import functools

import jax
import jax.numpy as jnp
from jax import lax
from jax.experimental import pallas as pl
from jax.experimental.pallas import tpu as pltpu
from jax.sharding import PartitionSpec as P

bf16 = jnp.bfloat16
f32 = jnp.float32
MIB = 1 << 20
ALL_MIB = 60

PLACES = 5
MOST = 8

VMEM = pl.BlockSpec(memory_space=pltpu.VMEM)
HBM = pl.BlockSpec(memory_space=pltpu.HBM)


def params(limit_mib):
    return pltpu.CompilerParams(vmem_limit_bytes=limit_mib * MIB)


def whole(shape):
    return pl.BlockSpec(shape, lambda *_: (0,) * len(shape))


def tile_at(i, size):
    return pl.ds(pl.multiple_of(i * size, size), size)


def beside(serving):
    across = jnp.broadcast_to(serving, (serving.shape[1],) * 2)
    return across.T, across


def cut_kernel(wide_rows, narrow, dp_size, limit, ids, serving, rows, out, cut, sems):
    groups, held, model = cut.shape
    dp_index = lax.axis_index("dp")
    first_narrow = wide_rows // dp_size
    rank = wide_rows // 3
    copies = []
    for e in range(groups):
        piece = e * dp_size + dp_index
        if e < first_narrow:
            spans = [(piece * model, 0, model)]
        else:
            q = piece - wide_rows
            spans = [
                (wide_rows * model + (g * rank + q) * narrow, g * narrow, narrow) for g in range(3)
            ]
        for source, target, width in spans:
            copies.append(
                pltpu.make_async_copy(
                    rows.at[:, pl.ds(pl.multiple_of(source, 128), width)],
                    cut.at[e, :, pl.ds(target, width)],
                    sems.at[len(copies)],
                )
            )
    for copy in copies:
        copy.start()
    mine, other = beside(serving[...])
    named = jnp.zeros((serving.shape[1], ids.shape[1]), f32)
    for k in range(ids.shape[0]):
        named = named + (mine[:, : ids.shape[1]] == ids[k : k + 1, :]).astype(f32)
    named = jnp.sum(named, axis=1, keepdims=True)
    holders = jnp.sum((mine == other).astype(f32), axis=1, keepdims=True)
    over = jnp.where((named > limit) & (holders < 2.0), 1.0, 0.0)
    over = jnp.max(over, axis=0, keepdims=True)
    for e in range(first_narrow, groups):
        cut[e, :, 3 * narrow :] = jnp.broadcast_to(over, (held, model - 3 * narrow)).astype(bf16)
    for copy in copies:
        copy.wait()
    for e in range(groups):
        out[e] = cut[e].reshape(out.shape[1:])


def cut_pieces(rows, ids, serving, limit, groups, dp_size, model, narrow, rank):
    held = rows.shape[0]
    wide_rows = 3 * rank
    first_narrow = wide_rows // dp_size
    return pl.pallas_call(
        functools.partial(cut_kernel, wide_rows, narrow, dp_size, limit),
        in_specs=[VMEM, VMEM, HBM],
        out_specs=VMEM,
        out_shape=jax.ShapeDtypeStruct((groups, held * model // 128, 128), bf16),
        scratch_shapes=[
            pltpu.VMEM((groups, held, model), bf16),
            pltpu.SemaphoreType.DMA((first_narrow + 3 * (groups - first_narrow),)),
        ],
        compiler_params=params(ALL_MIB),
        name="adapter_cut",
    )(ids, serving, rows)


def pick_kernel(held, flag_at, first_narrow, wanted, pieces, cells, out, rows):
    groups = pieces.shape[0]
    model = rows.shape[1]
    slots = out.shape[0]
    rows[...] = jnp.zeros_like(rows)
    for e in range(groups):
        rows[8 * e : 8 * e + held, :] = pieces[e].reshape(held, model).astype(f32)
    want = wanted[...]
    place = (want // held) * 8 + want % held
    chosen = lax.broadcasted_iota(jnp.int32, (8 * groups, slots), 0) == place
    picked = lax.dot_general(
        chosen.astype(bf16),
        rows[...].astype(bf16),
        (((0,), (0,)), ((), ())),
        preferred_element_type=f32,
    )
    flags = jnp.max(rows[:, flag_at : flag_at + 128], axis=0, keepdims=True)
    kept = picked[:, flag_at : flag_at + 128]
    flags = jnp.where(lax.axis_index("expert") >= first_narrow, jnp.broadcast_to(flags, kept.shape), kept)
    full = jnp.concatenate([picked[:, :flag_at], flags, picked[:, flag_at + 128 :]], axis=1)
    out[...] = full.astype(bf16).reshape(out.shape)


def pick_pieces(pieces, held, wanted, flag_at, first_narrow, cells):
    groups = pieces.shape[0]
    model = pieces.shape[1] * pieces.shape[2] // held
    slots, units, lanes = cells.shape
    row = model // lanes
    return pl.pallas_call(
        functools.partial(pick_kernel, held, flag_at, first_narrow),
        grid=(1,),
        in_specs=[whole((1, slots)), whole(pieces.shape), HBM],
        out_specs=pl.BlockSpec((slots, row, lanes), lambda i: (0, units // row - 1, 0)),
        out_shape=jax.ShapeDtypeStruct(cells.shape, bf16),
        input_output_aliases={2: 0},
        scratch_shapes=[pltpu.VMEM((8 * groups, model), f32)],
        compiler_params=params(ALL_MIB),
        name="adapter_pick",
    )(wanted.reshape(1, slots), pieces, cells)


def placement(ids, serving, places):
    tokens = ids.shape[1]
    mine, other = beside(serving)
    slots = mine.shape[0]
    below = lax.broadcasted_iota(jnp.int32, (slots, slots), 1) < lax.broadcasted_iota(
        jnp.int32, (slots, slots), 0
    )
    same = (mine == other).astype(f32)
    hot = jnp.sum(same, axis=1, keepdims=True) > 1.5
    second = jnp.sum(jnp.where(below, same, 0.0), axis=1, keepdims=True)
    named = mine[:, :tokens] == ids[0:1, :]
    for k in range(1, ids.shape[0]):
        named = named | (mine[:, :tokens] == ids[k : k + 1, :])
    before = lax.broadcasted_iota(jnp.int32, (tokens, tokens), 0) < lax.broadcasted_iota(
        jnp.int32, (tokens, tokens), 1
    )
    rank = jnp.dot(named.astype(bf16), before.astype(bf16), preferred_element_type=f32)
    rank = jnp.where(named, rank, -1.0)
    return [rank == jnp.where(hot, 2.0 * at + second, 1.0 * at) for at in places]


def dispatch_kernel(first, ids, serving, tokens, out, fills, sent, sems):
    places = fills.shape[0]
    slots, row, lanes = sent.shape[1:]
    masks = placement(ids[...], serving[...], range(first, first + places))
    for j in range(places):
        fills[j] = masks[j].astype(bf16)

    def send(j):
        return pltpu.make_async_copy(sent.at[j], out.at[:, tile_at(j, row), :], sems.at[j])

    @pl.loop(0, places)
    def _(j):
        part = jnp.dot(fills[j], tokens[...], preferred_element_type=f32).astype(bf16)
        sent[j] = part.reshape(slots, row, lanes)
        send(j).start()

    for j in range(places):
        send(j).wait()


def dispatch(ids, serving, tokens, first, places, spare):
    slots = serving.shape[1]
    count, model = tokens.shape
    row = model // 128
    return pl.pallas_call(
        functools.partial(dispatch_kernel, first),
        in_specs=[VMEM] * 3,
        out_specs=HBM,
        out_shape=jax.ShapeDtypeStruct((slots, (places + spare) * row, 128), bf16),
        scratch_shapes=[
            pltpu.VMEM((places, slots, count), bf16),
            pltpu.VMEM((places, slots, row, 128), bf16),
            pltpu.SemaphoreType.DMA((places,)),
        ],
        compiler_params=params(ALL_MIB),
        cost_estimate=pl.CostEstimate(
            flops=2 * places * slots * count * model,
            bytes_accessed=2 * places * slots * model,
            transcendentals=0,
        ),
        name="token_dispatch",
    )(ids, serving, tokens)


def expert_kernel(
    rank,
    factors_at,
    cells_hbm,
    factors_hbm,
    gate_hbm,
    up_hbm,
    down_hbm,
    out,
    cells,
    pieces,
    gate,
    up,
    down,
    x,
    factors,
    shrunk,
    hidden,
    sent,
    cell_sems,
    gate_sems,
    up_sems,
    down_sems,
    out_sems,
):
    slots = cells.shape[0]
    rows, model = x.shape
    units = hidden.shape[1]
    row = model // 128
    places = rows // slots
    tile = units // gate_sems.shape[0]
    width = sent.shape[2] * 128
    up_tiles, down_tiles = units // tile, model // width

    def load(i, source, target, size, sems):
        at = tile_at(i, size)
        return pltpu.make_async_copy(source.at[:, at], target.at[:, at], sems.at[i])

    def load_gate(i):
        return load(i, gate_hbm, gate, tile, gate_sems)

    def load_up(i):
        return load(i, up_hbm, up, tile, up_sems)

    def load_down(i):
        return load(i, down_hbm, down, width, down_sems)

    def send(i, j):
        at = pl.ds(pl.multiple_of(j * row + i * (width // 128), 8), width // 128)
        return pltpu.make_async_copy(sent.at[j], out.at[:, at, :], out_sems.at[i * places + j])

    def load_place(j):
        at = tile_at(j, row)
        return pltpu.make_async_copy(cells_hbm.at[:, at, :], cells.at[:, at, :], cell_sems.at[j])

    load_pieces = pltpu.make_async_copy(
        factors_hbm.at[:, pl.ds(factors_at * row, row), :], pieces, cell_sems.at[places]
    )
    load_pieces.start()
    for j in range(places):
        load_place(j).start()
    for i in range(up_tiles):
        load_gate(i).start()
        load_up(i).start()
    for i in range(down_tiles):
        load_down(i).start()

    load_pieces.wait()
    factors[...] = pieces[...].reshape(slots, model)

    @pl.loop(0, places)
    def _(j):
        here = tile_at(j, slots)
        load_place(j).wait()
        part = cells[:, tile_at(j, row), :].reshape(slots, model)
        x[here, :] = part
        shrunk[here, :] = lax.dot_general(
            part,
            factors[0 : 2 * rank, :],
            (((1,), (1,)), ((), ())),
            preferred_element_type=f32,
        ).astype(bf16)

    @pl.loop(0, up_tiles)
    def _(i):
        at = tile_at(i, tile)
        load_gate(i).wait()
        load_up(i).wait()
        into_gate = jnp.dot(x[...], gate[:, at], preferred_element_type=f32) + jnp.dot(
            shrunk[:, :rank], factors[3 * rank : 4 * rank, at], preferred_element_type=f32
        )
        up_at = pl.ds(pl.multiple_of(units + i * tile, tile), tile)
        into_up = jnp.dot(x[...], up[:, at], preferred_element_type=f32) + jnp.dot(
            shrunk[:, rank:], factors[3 * rank : 4 * rank, up_at], preferred_element_type=f32
        )
        hidden[:, at] = (into_gate / (1.0 + jnp.exp(-into_gate)) * into_up).astype(bf16)

    shrunk_down = lax.dot_general(
        hidden[...],
        factors[3 * rank : 4 * rank, 2 * units : 3 * units],
        (((1,), (1,)), ((), ())),
        preferred_element_type=f32,
    ).astype(bf16)

    @pl.loop(0, down_tiles)
    def _(i):
        at = tile_at(i, width)
        load_down(i).wait()
        total = jnp.dot(hidden[...], down[:, at], preferred_element_type=f32) + jnp.dot(
            shrunk_down, factors[2 * rank : 3 * rank, at], preferred_element_type=f32
        )
        for j in range(places):

            @pl.when(i > 0)
            def _():
                send(i - 1, j).wait()

            part = total[j * slots : (j + 1) * slots].astype(bf16)
            sent[j] = part.reshape(slots, width // 128, 128)
            send(i, j).start()

    for j in range(places):
        send(down_tiles - 1, j).wait()


def expert(cells, places, factors, factors_at, gate, up, down, rank):
    model, units = gate.shape
    slots = cells.shape[0]
    rows = slots * places
    row = model // 128
    tile, width = 256, 1024
    return pl.pallas_call(
        functools.partial(expert_kernel, rank, factors_at),
        in_specs=[HBM] * 5,
        out_specs=HBM,
        out_shape=jax.ShapeDtypeStruct((slots, places * row, 128), bf16),
        scratch_shapes=[
            pltpu.VMEM((slots, places * row, 128), bf16),
            pltpu.VMEM((slots, row, 128), bf16),
            pltpu.VMEM((model, units), bf16),
            pltpu.VMEM((model, units), bf16),
            pltpu.VMEM((units, model), bf16),
            pltpu.VMEM((rows, model), bf16),
            pltpu.VMEM((slots, model), bf16),
            pltpu.VMEM((rows, 2 * rank), bf16),
            pltpu.VMEM((rows, units), bf16),
            pltpu.VMEM((places, slots, width // 128, 128), bf16),
            pltpu.SemaphoreType.DMA((places + 1,)),
            pltpu.SemaphoreType.DMA((units // tile,)),
            pltpu.SemaphoreType.DMA((units // tile,)),
            pltpu.SemaphoreType.DMA((model // width,)),
            pltpu.SemaphoreType.DMA((places * (model // width),)),
        ],
        compiler_params=params(ALL_MIB),
        cost_estimate=pl.CostEstimate(
            flops=6 * rows * model * units,
            bytes_accessed=6 * model * units + 4 * rows * model,
            transcendentals=rows * units,
        ),
        name="slot_expert",
    )(cells, factors, gate, up, down)


def combine_kernel(first, ids, weight, serving, answers, *rest):
    sems, block, cells, out = rest[-1], rest[-2], rest[-3], rest[-4]
    count, model = out.shape
    rows, width = block.shape
    slots = cells.shape[0]
    places = rows // slots
    row = model // 128

    def load(i, j):
        at = pl.ds(pl.multiple_of(j * row + i * (width // 128), width // 128), width // 128)
        return pltpu.make_async_copy(answers.at[:, at, :], cells.at[:, at, :], sems.at[i * places + j])

    for i in range(model // width):
        for j in range(places):
            load(i, j).start()
    mine, _ = beside(serving[...])
    given = jnp.zeros((slots, count), f32)
    for k in range(ids.shape[0]):
        given = given + jnp.where(mine[:, :count] == ids[k : k + 1, :], weight[k : k + 1, :], 0.0)
    parts = []
    for mask in placement(ids[...], serving[...], range(first, first + places)):
        part = jnp.where(mask, given, 0.0)
        high = part.astype(bf16).astype(f32)
        parts.append(jnp.concatenate([high, part - high], axis=1).T)
    both = jnp.concatenate(parts, axis=1).astype(bf16)

    @pl.loop(0, model // width)
    def _(i):
        at = tile_at(i, width)
        for j in range(places):
            load(i, j).wait()
            units = pl.ds(pl.multiple_of(j * row + i * (width // 128), width // 128), width // 128)
            block[j * slots : (j + 1) * slots, :] = cells[:, units, :].reshape(slots, width)
        total = jnp.dot(both, block[...], preferred_element_type=f32)
        total = total[:count] + total[count:]
        if len(rest) == 5:
            total = total + rest[0][:, at]
        out[:, at] = total.astype(out.dtype)


def combine(ids, weight, serving, first, answers, model, before=None, kind=f32):
    count = ids.shape[1]
    slots, units, lanes = answers.shape

    places = units * lanes // model
    width = 2048
    more = () if before is None else (before,)
    return pl.pallas_call(
        functools.partial(combine_kernel, first),
        grid=(1,),
        in_specs=[VMEM] * 3 + [HBM] + [VMEM] * len(more),
        out_specs=whole((count, model)),
        out_shape=jax.ShapeDtypeStruct((count, model), kind),
        scratch_shapes=[
            pltpu.VMEM(answers.shape, bf16),
            pltpu.VMEM((places * slots, width), bf16),
            pltpu.SemaphoreType.DMA((places * (model // width),)),
        ],
        compiler_params=params(ALL_MIB),
        cost_estimate=pl.CostEstimate(
            flops=4 * count * places * slots * model,
            bytes_accessed=2 * places * slots * model,
            transcendentals=0,
        ),
        name="token_combine",
    )(ids, weight, serving, answers, *more)


def body(
    tokens,
    routed,
    weight,
    serving,
    gate,
    up,
    down,
    trainer_order,
    trainer_rows,
):
    groups = lax.axis_size("expert")
    dp_size = lax.axis_size("dp")
    slots = serving.shape[0]
    experts = trainer_order.shape[0]
    held, packed = trainer_rows.shape
    count, model = tokens.shape
    units = gate.shape[2]
    rank = packed // (3 * (model + units))
    first_narrow = 3 * rank // dp_size
    ids, weight, serving_row = routed.T, weight.T, serving.reshape(1, slots)

    def there(cells):
        return lax.all_to_all(cells, ("expert", "dp"), split_axis=0, concat_axis=0, tiled=True)

    mine = cut_pieces(
        trainer_rows, ids, serving_row, PLACES, groups, dp_size, model, units, rank
    )
    spread = lax.all_to_all(mine, "expert", split_axis=0, concat_axis=0, tiled=True)
    trainer_row = jnp.sum(
        jnp.where(
            serving[:, None] == trainer_order[None, :],
            jnp.arange(experts, dtype=jnp.int32)[None, :],
            0,
        ),
        axis=1,
    )
    sent = dispatch(ids, serving_row, tokens, 0, PLACES, 1)
    cells = there(pick_pieces(spread, held, trainer_row, 3 * units, first_narrow, sent))

    def answer(tokens_in, places):
        return there(expert(tokens_in, places, cells, PLACES, gate[0], up[0], down[0], rank))

    answers = answer(cells, PLACES)
    flags = cells[3 * rank :, PLACES * model // 128 + 3 * units // 128, 0]

    def one_round():
        return combine(ids, weight, serving_row, 0, answers, model, None, bf16)

    def two_rounds():
        total = combine(ids, weight, serving_row, 0, answers, model)
        places = MOST - PLACES
        more = there(dispatch(ids, serving_row, tokens, PLACES, places, 0))
        more = answer(more, places)
        return combine(ids, weight, serving_row, PLACES, more, model, total, bf16)

    return lax.cond(jnp.max(flags.astype(f32)) > 0.0, two_rounds, one_round)


def solution(mesh):
    split = P(("expert", "dp"), None)
    slot = P(("expert", "dp"), None, None)
    placed = (split, split, split, P(), slot, slot, slot, P(), P("expert", None))
    return jax.shard_map(body, mesh=mesh, in_specs=placed, out_specs=split, check_vma=False)
```

```python
import functools

import jax
import jax.numpy as jnp
from jax import lax
from jax.experimental import pallas as pl
from jax.experimental.pallas import tpu as pltpu
from jax.sharding import PartitionSpec as P

bf16 = jnp.bfloat16
f32 = jnp.float32
ALL_BYTES = 63_400_000
MOST_BYTES = 55 << 20

PLACES = 5
MOST = 8

VMEM = pl.BlockSpec(memory_space=pltpu.VMEM)
HBM = pl.BlockSpec(memory_space=pltpu.HBM)


def params(limit):
    return pltpu.CompilerParams(vmem_limit_bytes=limit)


def whole(shape):
    return pl.BlockSpec(shape, lambda *_: (0,) * len(shape))


def tile_at(i, size):
    return pl.ds(pl.multiple_of(i * size, size), size)


def beside(serving):
    across = jnp.broadcast_to(serving, (serving.shape[1],) * 2)
    return across.T, across


def cut_kernel(wide_rows, narrow, dp_size, limit, ids, serving, rows, out, cut, flat, sems, out_sems):
    groups, held, model = cut.shape
    dp_index = lax.axis_index("dp")
    first_narrow = wide_rows // dp_size
    rank = wide_rows // 3
    copies = []
    owners = []
    for e in range(groups):
        piece = e * dp_size + dp_index
        if e < first_narrow:
            spans = [(piece * model, 0, model)]
        else:
            q = piece - wide_rows
            spans = [
                (wide_rows * model + (g * rank + q) * narrow, g * narrow, narrow) for g in range(3)
            ]
        for source, target, width in spans:
            owners.append(e)
            copies.append(
                pltpu.make_async_copy(
                    rows.at[:, pl.ds(pl.multiple_of(source, 128), width)],
                    cut.at[e, :, pl.ds(target, width)],
                    sems.at[len(copies)],
                )
            )
    for copy in copies:
        copy.start()
    mine, other = beside(serving[...])
    named = jnp.zeros((serving.shape[1], ids.shape[1]), f32)
    for k in range(ids.shape[0]):
        named = named + (mine[:, : ids.shape[1]] == ids[k : k + 1, :]).astype(f32)
    named = jnp.sum(named, axis=1, keepdims=True)
    holders = jnp.sum((mine == other).astype(f32), axis=1, keepdims=True)
    over = jnp.where((named > limit) & (holders < 2.0), 1.0, 0.0)
    over = jnp.max(over, axis=0, keepdims=True)
    for e in range(first_narrow, groups):
        cut[e, :, 3 * narrow :] = jnp.broadcast_to(over, (held, model - 3 * narrow)).astype(bf16)
    sends = []
    for e in range(groups):
        for copy, owner in zip(copies, owners):
            if owner == e:
                copy.wait()
        flat[e] = cut[e].reshape(flat.shape[1:])
        sends.append(pltpu.make_async_copy(flat.at[e], out.at[e], out_sems.at[e]))
        sends[e].start()
    for send in sends:
        send.wait()


def cut_pieces(rows, ids, serving, limit, groups, dp_size, model, narrow, rank):
    held = rows.shape[0]
    wide_rows = 3 * rank
    first_narrow = wide_rows // dp_size
    return pl.pallas_call(
        functools.partial(cut_kernel, wide_rows, narrow, dp_size, limit),
        in_specs=[VMEM, VMEM, HBM],
        out_specs=HBM,
        out_shape=jax.ShapeDtypeStruct((groups, held * model // 128, 128), bf16),
        scratch_shapes=[
            pltpu.VMEM((groups, held, model), bf16),
            pltpu.VMEM((groups, held * model // 128, 128), bf16),
            pltpu.SemaphoreType.DMA((first_narrow + 3 * (groups - first_narrow),)),
            pltpu.SemaphoreType.DMA((groups,)),
        ],
        compiler_params=params(ALL_BYTES),
        name="adapter_cut",
    )(ids, serving, rows)


def pick_kernel(held, flag_at, first_narrow, wanted, pieces, cells, out, rows, sent, sems):
    groups = pieces.shape[0]
    model = rows.shape[1]
    slots = sent.shape[1]
    rows[...] = jnp.zeros_like(rows)
    for e in range(groups):
        rows[8 * e : 8 * e + held, :] = pieces[e].reshape(held, model).astype(f32)
    want = wanted[...]
    place = (want // held) * 8 + want % held
    chosen = lax.broadcasted_iota(jnp.int32, (8 * groups, slots), 0) == place
    chosen = chosen.astype(bf16)
    parts = sems.shape[0]
    width = model // parts
    copies = []
    for c in range(parts):
        part = rows[:, c * width : (c + 1) * width]
        picked = lax.dot_general(
            chosen,
            part.astype(bf16),
            (((0,), (0,)), ((), ())),
            preferred_element_type=f32,
        )
        if flag_at // width == c:
            at = flag_at % width
            flags = jnp.max(part[:, at : at + 128], axis=0, keepdims=True)
            kept = picked[:, at : at + 128]
            flags = jnp.where(
                lax.axis_index("expert") >= first_narrow, jnp.broadcast_to(flags, kept.shape), kept
            )
            picked = jnp.concatenate([picked[:, :at], flags, picked[:, at + 128 :]], axis=1)
        sent[c] = picked.astype(bf16).reshape(sent.shape[1:])
        at = out.shape[1] - (parts - c) * (width // 128)
        copies.append(
            pltpu.make_async_copy(sent.at[c], out.at[:, pl.ds(at, width // 128), :], sems.at[c])
        )
        copies[c].start()
    for copy in copies:
        copy.wait()


def pick_pieces(pieces, held, wanted, flag_at, first_narrow, cells):
    groups = pieces.shape[0]
    model = pieces.shape[1] * pieces.shape[2] // held
    slots, _, lanes = cells.shape
    return pl.pallas_call(
        functools.partial(pick_kernel, held, flag_at, first_narrow),
        in_specs=[VMEM, VMEM, HBM],
        out_specs=HBM,
        out_shape=jax.ShapeDtypeStruct(cells.shape, bf16),
        input_output_aliases={2: 0},
        scratch_shapes=[
            pltpu.VMEM((8 * groups, model), f32),
            pltpu.VMEM((4, slots, model // 4 // lanes, lanes), bf16),
            pltpu.SemaphoreType.DMA((4,)),
        ],
        compiler_params=params(MOST_BYTES),
        name="adapter_pick",
    )(wanted.reshape(1, slots), pieces, cells)


def placement(ids, serving, places):
    tokens = ids.shape[1]
    mine, other = beside(serving)
    slots = mine.shape[0]
    below = lax.broadcasted_iota(jnp.int32, (slots, slots), 1) < lax.broadcasted_iota(
        jnp.int32, (slots, slots), 0
    )
    same = (mine == other).astype(f32)
    hot = jnp.sum(same, axis=1, keepdims=True) > 1.5
    second = jnp.sum(jnp.where(below, same, 0.0), axis=1, keepdims=True)
    named = mine[:, :tokens] == ids[0:1, :]
    for k in range(1, ids.shape[0]):
        named = named | (mine[:, :tokens] == ids[k : k + 1, :])
    before = lax.broadcasted_iota(jnp.int32, (tokens, tokens), 0) < lax.broadcasted_iota(
        jnp.int32, (tokens, tokens), 1
    )
    rank = jnp.dot(named.astype(bf16), before.astype(bf16), preferred_element_type=f32)
    rank = jnp.where(named, rank, -1.0)
    return [rank == jnp.where(hot, 2.0 * at + second, 1.0 * at) for at in places]


def dispatch_kernel(first, ids, serving, tokens, out, fills, sent, sems):
    places = fills.shape[0]
    slots, row, lanes = sent.shape[1:]
    masks = placement(ids[...], serving[...], range(first, first + places))
    for j in range(places):
        fills[j] = masks[j].astype(bf16)

    def send(j):
        return pltpu.make_async_copy(sent.at[j], out.at[:, tile_at(j, row), :], sems.at[j])

    @pl.loop(0, places)
    def _(j):
        part = jnp.dot(fills[j], tokens[...], preferred_element_type=f32).astype(bf16)
        sent[j] = part.reshape(slots, row, lanes)
        send(j).start()

    for j in range(places):
        send(j).wait()


def dispatch(ids, serving, tokens, first, places, spare):
    slots = serving.shape[1]
    count, model = tokens.shape
    row = model // 128
    return pl.pallas_call(
        functools.partial(dispatch_kernel, first),
        in_specs=[VMEM] * 3,
        out_specs=HBM,
        out_shape=jax.ShapeDtypeStruct((slots, (places + spare) * row, 128), bf16),
        scratch_shapes=[
            pltpu.VMEM((places, slots, count), bf16),
            pltpu.VMEM((places, slots, row, 128), bf16),
            pltpu.SemaphoreType.DMA((places,)),
        ],
        compiler_params=params(ALL_BYTES),
        cost_estimate=pl.CostEstimate(
            flops=2 * places * slots * count * model,
            bytes_accessed=2 * places * slots * model,
            transcendentals=0,
        ),
        name="token_dispatch",
    )(ids, serving, tokens)


def expert_kernel(
    rank,
    factors_at,
    cells_hbm,
    factors_hbm,
    gate_hbm,
    up_hbm,
    down_hbm,
    out,
    cells,
    pieces,
    gate,
    up,
    down,
    x,
    factors,
    shrunk,
    hidden,
    sent,
    cell_sems,
    gate_sems,
    up_sems,
    down_sems,
    out_sems,
):
    slots = cells.shape[0]
    rows, model = x.shape
    units = hidden.shape[1]
    row = model // 128
    places = rows // slots
    tile = units // gate_sems.shape[0]
    width = sent.shape[2] * 128
    up_tiles, down_tiles = units // tile, model // width

    def load(i, source, target, size, sems):
        at = tile_at(i, size)
        return pltpu.make_async_copy(source.at[:, at], target.at[:, at], sems.at[i])

    def load_gate(i):
        return load(i, gate_hbm, gate, tile, gate_sems)

    def load_up(i):
        return load(i, up_hbm, up, tile, up_sems)

    def load_down(i):
        return load(i, down_hbm, down, width, down_sems)

    def send(i, j):
        at = pl.ds(pl.multiple_of(j * row + i * (width // 128), 8), width // 128)
        return pltpu.make_async_copy(sent.at[j], out.at[:, at, :], out_sems.at[i * places + j])

    def load_place(j):
        at = tile_at(j, row)
        return pltpu.make_async_copy(cells_hbm.at[:, at, :], cells.at[:, at, :], cell_sems.at[j])

    load_pieces = pltpu.make_async_copy(
        factors_hbm.at[:, pl.ds(factors_at * row, row), :], pieces, cell_sems.at[places]
    )
    load_pieces.start()
    for j in range(places):
        load_place(j).start()
    for i in range(up_tiles):
        load_gate(i).start()
        load_up(i).start()
    for i in range(down_tiles):
        load_down(i).start()

    load_pieces.wait()
    factors[...] = pieces[...].reshape(slots, model)

    @pl.loop(0, places)
    def _(j):
        here = tile_at(j, slots)
        load_place(j).wait()
        part = cells[:, tile_at(j, row), :].reshape(slots, model)
        x[here, :] = part
        shrunk[here, :] = lax.dot_general(
            part,
            factors[0 : 2 * rank, :],
            (((1,), (1,)), ((), ())),
            preferred_element_type=f32,
        ).astype(bf16)

    @pl.loop(0, up_tiles)
    def _(i):
        at = tile_at(i, tile)
        load_gate(i).wait()
        load_up(i).wait()
        into_gate = jnp.dot(x[...], gate[:, at], preferred_element_type=f32) + jnp.dot(
            shrunk[:, :rank], factors[3 * rank : 4 * rank, at], preferred_element_type=f32
        )
        up_at = pl.ds(pl.multiple_of(units + i * tile, tile), tile)
        into_up = jnp.dot(x[...], up[:, at], preferred_element_type=f32) + jnp.dot(
            shrunk[:, rank:], factors[3 * rank : 4 * rank, up_at], preferred_element_type=f32
        )
        hidden[:, at] = (into_gate / (1.0 + jnp.exp(-into_gate)) * into_up).astype(bf16)

    shrunk_down = lax.dot_general(
        hidden[...],
        factors[3 * rank : 4 * rank, 2 * units : 3 * units],
        (((1,), (1,)), ((), ())),
        preferred_element_type=f32,
    ).astype(bf16)

    @pl.loop(0, down_tiles)
    def _(i):
        at = tile_at(i, width)
        load_down(i).wait()
        total = jnp.dot(hidden[...], down[:, at], preferred_element_type=f32) + jnp.dot(
            shrunk_down, factors[2 * rank : 3 * rank, at], preferred_element_type=f32
        )
        for j in range(places):

            @pl.when(i > 0)
            def _():
                send(i - 1, j).wait()

            part = total[j * slots : (j + 1) * slots].astype(bf16)
            sent[j] = part.reshape(slots, width // 128, 128)
            send(i, j).start()

    for j in range(places):
        send(down_tiles - 1, j).wait()


def expert(cells, places, factors, factors_at, gate, up, down, rank):
    model, units = gate.shape
    slots = cells.shape[0]
    rows = slots * places
    row = model // 128
    tile, width = 256, 1024
    return pl.pallas_call(
        functools.partial(expert_kernel, rank, factors_at),
        in_specs=[HBM] * 5,
        out_specs=HBM,
        out_shape=jax.ShapeDtypeStruct((slots, places * row, 128), bf16),
        scratch_shapes=[
            pltpu.VMEM((slots, places * row, 128), bf16),
            pltpu.VMEM((slots, row, 128), bf16),
            pltpu.VMEM((model, units), bf16),
            pltpu.VMEM((model, units), bf16),
            pltpu.VMEM((units, model), bf16),
            pltpu.VMEM((rows, model), bf16),
            pltpu.VMEM((slots, model), bf16),
            pltpu.VMEM((rows, 2 * rank), bf16),
            pltpu.VMEM((rows, units), bf16),
            pltpu.VMEM((places, slots, width // 128, 128), bf16),
            pltpu.SemaphoreType.DMA((places + 1,)),
            pltpu.SemaphoreType.DMA((units // tile,)),
            pltpu.SemaphoreType.DMA((units // tile,)),
            pltpu.SemaphoreType.DMA((model // width,)),
            pltpu.SemaphoreType.DMA((places * (model // width),)),
        ],
        compiler_params=params(ALL_BYTES),
        cost_estimate=pl.CostEstimate(
            flops=6 * rows * model * units,
            bytes_accessed=6 * model * units + 4 * rows * model,
            transcendentals=rows * units,
        ),
        name="slot_expert",
    )(cells, factors, gate, up, down)


def weights_kernel(first, ids, weight, serving, after, out):
    slots, count = serving.shape[1], ids.shape[1]
    places = out.shape[1] // slots
    mine, _ = beside(serving[...])
    given = jnp.zeros((slots, count), f32)
    for k in range(ids.shape[0]):
        given = given + jnp.where(mine[:, :count] == ids[k : k + 1, :], weight[k : k + 1, :], 0.0)
    parts = []
    for mask in placement(ids[...], serving[...], range(first, first + places)):
        part = jnp.where(mask, given, 0.0)
        high = part.astype(bf16).astype(f32)
        parts.append(jnp.concatenate([high, part - high], axis=1).T)
    out[...] = jnp.concatenate(parts, axis=1).astype(bf16)


def combine_weights(ids, weight, serving, first, places, after):
    shape = (2 * ids.shape[1], places * serving.shape[1])
    return pl.pallas_call(
        functools.partial(weights_kernel, first),
        in_specs=[VMEM] * 3 + [HBM],
        out_specs=VMEM,
        out_shape=jax.ShapeDtypeStruct(shape, bf16),
        name="combine_weights",
    )(ids, weight, serving, after)


def combine_kernel(both, answers, *rest):
    sems, block, cells, out = rest[-1], rest[-2], rest[-3], rest[-4]
    count, model = out.shape
    rows, width = block.shape
    slots = cells.shape[0]
    places = rows // slots
    row = model // 128

    def load(i, j):
        at = pl.ds(pl.multiple_of(j * row + i * (width // 128), width // 128), width // 128)
        return pltpu.make_async_copy(answers.at[:, at, :], cells.at[:, at, :], sems.at[i * places + j])

    for i in range(model // width):
        for j in range(places):
            load(i, j).start()

    @pl.loop(0, model // width)
    def _(i):
        at = tile_at(i, width)
        for j in range(places):
            load(i, j).wait()
            units = pl.ds(pl.multiple_of(j * row + i * (width // 128), width // 128), width // 128)
            block[j * slots : (j + 1) * slots, :] = cells[:, units, :].reshape(slots, width)
        total = jnp.dot(both[...], block[...], preferred_element_type=f32)
        total = total[:count] + total[count:]
        if len(rest) == 5:
            total = total + rest[0][:, at]
        out[:, at] = total.astype(out.dtype)


def combine(both, answers, model, before=None, kind=f32):
    count = both.shape[0] // 2
    slots, units, lanes = answers.shape

    places = units * lanes // model
    width = 2048
    more = () if before is None else (before,)
    return pl.pallas_call(
        combine_kernel,
        grid=(1,),
        in_specs=[VMEM, HBM] + [VMEM] * len(more),
        out_specs=whole((count, model)),
        out_shape=jax.ShapeDtypeStruct((count, model), kind),
        scratch_shapes=[
            pltpu.VMEM(answers.shape, bf16),
            pltpu.VMEM((places * slots, width), bf16),
            pltpu.SemaphoreType.DMA((places * (model // width),)),
        ],
        compiler_params=params(ALL_BYTES),
        cost_estimate=pl.CostEstimate(
            flops=4 * count * places * slots * model,
            bytes_accessed=2 * places * slots * model,
            transcendentals=0,
        ),
        name="token_combine",
    )(both, answers, *more)


def body(
    tokens,
    routed,
    weight,
    serving,
    gate,
    up,
    down,
    trainer_order,
    trainer_rows,
):
    groups = lax.axis_size("expert")
    dp_size = lax.axis_size("dp")
    slots = serving.shape[0]
    experts = trainer_order.shape[0]
    held, packed = trainer_rows.shape
    count, model = tokens.shape
    units = gate.shape[2]
    rank = packed // (3 * (model + units))
    first_narrow = 3 * rank // dp_size
    ids, weight, serving_row = routed.T, weight.T, serving.reshape(1, slots)

    def there(cells):
        return lax.all_to_all(cells, ("expert", "dp"), split_axis=0, concat_axis=0, tiled=True)

    mine = cut_pieces(
        trainer_rows, ids, serving_row, PLACES, groups, dp_size, model, units, rank
    )
    spread = lax.all_to_all(mine, "expert", split_axis=0, concat_axis=0, tiled=True)
    trainer_row = jnp.sum(
        jnp.where(
            serving[:, None] == trainer_order[None, :],
            jnp.arange(experts, dtype=jnp.int32)[None, :],
            0,
        ),
        axis=1,
    )
    sent = dispatch(ids, serving_row, tokens, 0, PLACES, 1)
    cells = there(pick_pieces(spread, held, trainer_row, 3 * units, first_narrow, sent))

    def answer(tokens_in, places):
        return there(expert(tokens_in, places, cells, PLACES, gate[0], up[0], down[0], rank))

    answers = answer(cells, PLACES)
    flags = cells[3 * rank :, PLACES * model // 128 + 3 * units // 128, 0]

    both = combine_weights(ids, weight, serving_row, 0, PLACES, cells)

    def one_round():
        return combine(both, answers, model, None, bf16)

    def two_rounds():
        total = combine(both, answers, model)
        places = MOST - PLACES
        more = there(dispatch(ids, serving_row, tokens, PLACES, places, 0))
        more = answer(more, places)
        after = combine_weights(ids, weight, serving_row, PLACES, places, more)
        return combine(after, more, model, total, bf16)

    return lax.cond(jnp.max(flags.astype(f32)) > 0.0, two_rounds, one_round)


def solution(mesh):
    split = P(("expert", "dp"), None)
    slot = P(("expert", "dp"), None, None)
    placed = (split, split, split, P(), slot, slot, slot, P(), P("expert", None))
    return jax.shard_map(body, mesh=mesh, in_specs=placed, out_specs=split, check_vma=False)
```
